32 devices in a mesh: aux: 4 (over y, core), virt: 8 (over z, x).
Axes of the slice: x: 2, y: 2, z: 4, core: 2. Of those that a mesh axis runs over, the one named last changes fastest.
Arguments:
- row_codes: bfloat16 [4, 128, 1920], P('aux'), may hold values from -4 to 4
- row_scales: float32 [4, 128, 15], P('aux'), may hold values from 0.2 to 2
- panel_codes: bfloat16 [4, 1920, 1920], P('aux', 'virt'), may hold values from -4 to 4
- panel_scales: float32 [4, 1920, 15], P('aux', 'virt'), may hold values from 0.0034232659 to 0.03423266
- amplitudes: bfloat16 [16, 1920, 1920], P('aux', 'virt'), may hold values from -0.125 to 0.125
Outputs:
- residual: float32 [1920, 16, 128], P('virt', 'aux')
The draws below stay inside these ranges and needn't reach their ends.
All inputs are finite; a program needn't handle non-finite values.
Results may differ from the reference program's by a relative error of at most 0.005.
Values may be sent and summed in bfloat16 or wider, within the bound.
A program may use at most 128 MiB of HBM per device.

```python
import math
import jax
import jax.numpy as jnp
from jax import lax

V = 1920
BLK = 128
AW = 128
NQ = 4
NPAIRS = 16
NBLK = 15


def spiked(values, key, source, target, blocks, factor):
    owner, partner = [(jnp.arange(values.shape[axis_at]) // (values.shape[axis_at] // blocks)).reshape([-1 if axis == axis_at else 1 for axis in range(values.ndim)]) for axis_at in (source, target)]
    chosen = jax.random.permutation(key, blocks)[partner]
    strong = (owner == chosen) | (owner == (partner + blocks // 2) % blocks)
    return jnp.where(strong, factor * values, values)


def levels(rng, shape, split, low, high):
    def one(dim, shards_of):
        draws = jax.random.uniform(jax.random.fold_in(jax.random.fold_in(rng, 6), dim), (shards_of,), jnp.float32, low / len(split), high / len(split))
        return jnp.repeat(jnp.exp(draws), shape[dim] // shards_of).reshape((-1,) + (1,) * (len(shape) - dim - 1))

    factor_of = one(*split[0])
    for cut in split[1:]:
        factor_of = factor_of * one(*cut)
    return factor_of


def scatter_about(key, shape, spread, reach, cuts=(), held_as=jnp.bfloat16):
    drawn = jax.random.normal(key, shape, jnp.float32) * spread
    if len(cuts) > 0:
        drawn = levels(key, shape, cuts, -0.22, 0.18) * drawn
    return jnp.clip(drawn, min=-reach, max=reach).astype(held_as)


def noise_with(own_key, extent, spread, most, pieces, heavy, kind=jnp.bfloat16):
    drawn = spread * jax.random.normal(own_key, extent, jnp.float32)
    if pieces:
        drawn = drawn * levels(own_key, extent, pieces, -0.22, 0.18)
    return jnp.clip(spiked(drawn, jax.random.fold_in(own_key, 3), *heavy), -most, most).astype(kind)


def setup_inputs(seed: int = 0) -> dict:
    key_list = jax.random.split(jax.random.key(seed), 6)
    return {
        "row_codes": scatter_about(key_list[0], (NQ, AW, V), 1.0, 4.0, ((0, 4),)),
        "row_scales": jnp.clip(jnp.exp(math.log(2.0) - 2.3025851 * jax.random.uniform(key_list[1], (NQ, AW, NBLK), jnp.float32) ** levels(key_list[1], (NQ, AW, NBLK), ((0, 4),), -0.2, 0.2)), 0.2, 2.0),
        "panel_codes": noise_with(key_list[2], (NQ, V, V), 1.0, 4.0, ((0, 4), (1, 8)), (1, 2, 8, 2.0)),
        "panel_scales": jnp.clip(jnp.exp(math.log(0.03423266) - 2.3025852 * jax.random.uniform(key_list[3], (NQ, V, NBLK), jnp.float32) ** levels(key_list[3], (NQ, V, NBLK), ((0, 4), (1, 8)), -0.2, 0.2)), 0.0034232659, 0.03423266),
        "amplitudes": scatter_about(key_list[4], (NPAIRS, V, V), V ** -0.5, 0.125, ((0, 4), (1, 8))),
    }


def reference(row_codes, row_scales, panel_codes, panel_scales, amplitudes):
    row_decoded = (row_codes.astype(jnp.float32).reshape(NQ, AW, NBLK, BLK) * row_scales[:, :, :, None]).reshape(NQ, AW, V).astype(jnp.bfloat16)
    panel_decoded = (panel_codes.astype(jnp.float32).reshape(NQ, V, NBLK, BLK) * panel_scales[:, :, :, None]).reshape(NQ, V, V).astype(jnp.bfloat16)
    row_wide = row_decoded.astype(jnp.float32)
    panel_wide = panel_decoded.astype(jnp.float32)

    def one_pair(amp):
        half = jnp.einsum("qac,dc->qda", row_wide, amp.astype(jnp.float32)).astype(jnp.bfloat16)
        return jnp.einsum("qdb,qda->ba", panel_wide, half.astype(jnp.float32))

    result = lax.map(one_pair, amplitudes)
    return jnp.transpose(result, (1, 0, 2))
```

```python
import functools

import jax
import jax.numpy as jnp
from jax import lax
from jax.experimental import pallas as pl
from jax.experimental.pallas import tpu as pltpu
from jax.sharding import PartitionSpec as P

MESH = pl.DeviceIdType.MESH
BF16 = jnp.bfloat16
F32 = jnp.float32


def kernel(
    na, nhi, nlo,
    rowc, rows_, panc, pans, amp_hbm, out,
    rowbuf, pg, half, amp, own, xs, xr, zs, zr,
    amp_sem, row0, ry, rx, rm, pm, py, pf, xsem, zsem,
):
    npair, d, length = amp.shape
    width = rowc.shape[1]
    blocks = rows_.shape[2]
    blk = length // blocks
    dp = pg.shape[3]
    bw = pg.shape[2]
    ny = na // 2
    nw = nhi * nlo
    part = width // nlo

    i = lax.axis_index("aux")
    j = lax.axis_index("virt")
    chip, core = i // 2, i % 2
    hi, lo = j // nlo, j % nlo
    mate_i = chip * 2 + (1 - core)

    def chip_at(o):
        return lax.rem(chip + o + ny, ny)

    def lo_at(s):
        return lax.rem(lo + s + nlo, nlo)

    def hi_at(t):
        return lax.rem(hi + t + nhi, nhi)

    mate = (mate_i, j)

    def over(o):
        return (chip_at(o) * 2 + core, j)

    def beside(s):
        return (i, hi * nlo + lo_at(s))

    def along(t):
        return (i, hi_at(t) * nlo + lo)

    amp_in = pltpu.make_async_copy(amp_hbm, amp, amp_sem)
    amp_in.start()

    barrier = pltpu.get_barrier_semaphore()
    partners = [mate] + [over(o) for o in range(1, ny)]
    partners += [beside(s) for s in range(1, nlo)] + [along(t) for t in range(1, nhi)]
    for who in partners:
        pl.semaphore_signal(barrier, inc=1, device_id=who, device_id_type=MESH)

    my_row = pl.multiple_of(i * width, width)
    for k in range(blocks):
        at = slice(k * blk, (k + 1) * blk)
        rowbuf[pl.ds(my_row, width), at] = (
            rowc[0, :, at].astype(F32) * rows_[0, :, k : k + 1]
        ).astype(BF16)

    pl.semaphore_wait(barrier, len(partners))

    def send(ref, sems, who):
        return pltpu.make_async_remote_copy(
            src_ref=ref, dst_ref=ref, send_sem=sems[0], recv_sem=sems[1],
            device_id=who, device_id_type=MESH,
        )

    def piece(q, p):
        return rowbuf.at[pl.ds(pl.multiple_of(q * width + p * part, part), part)]

    def row_mate(q):
        ref = rowbuf.at[pl.ds(pl.multiple_of(q * width, width), width)]
        return send(ref, (row0.at[0], row0.at[1]), mate)

    def row_over(o, q):
        return send(piece(q, lo), (ry.at[0, o], ry.at[1, o]), over(o))

    def row_beside(o, s, p):
        q = chip_at(-o) * 2 + core
        return send(piece(q, p), (rx.at[0, o, s], rx.at[1, o, s]), beside(s))

    def row_fwd(o, s, c):
        q = chip_at(-o) * 2 + c
        return send(piece(q, lo_at(-s)), (rm.at[0, o, s], rm.at[1, o, s]), mate)

    row_mate(i).start()
    for o in range(1, ny):
        row_over(o, i).start()

    half[...] = jnp.zeros_like(half)
    for k in range(blocks):
        at = slice(k * blk, (k + 1) * blk)
        dec = panc[0, :, at].astype(F32) * pans[0, :, k : k + 1]
        if dp > d:
            dec = jnp.concatenate([dec, jnp.zeros((dp - d, blk), F32)], axis=0)
        turned = dec.T
        first = k * blk
        while first < (k + 1) * blk:
            c = first // bw
            last = min((c + 1) * bw, (k + 1) * blk)
            pg[i, c, first - c * bw : last - c * bw, :] = turned[
                first - k * blk : last - k * blk
            ].astype(BF16)
            first = last

    def block_of(t, s):
        return hi_at(t) * nlo + lo_at(s)

    def pan_mate(q, t, s):
        n = (t - 1) * nlo + (s - 1)
        return send(pg.at[q, block_of(t, s)], (pm.at[0, n], pm.at[1, n]), mate)

    def pan_over(o, q, t, s):
        n = (t - 1) * nlo + (s - 1)
        return send(pg.at[q, block_of(t, s)], (py.at[0, o, n], py.at[1, o, n]), over(o))

    def pan_fwd(o, c, t, s):
        n = (t - 1) * nlo + (s - 1)
        q = chip_at(-o) * 2 + c
        return send(pg.at[q, block_of(t, s)], (pf.at[0, o, n], pf.at[1, o, n]), mate)

    for t in range(1, nhi + 1):
        for s in range(1, nlo + 1):
            for o in range(1, ny):
                pan_over(o, i, t, s).start()
            pan_mate(i, t, s).start()

    def half_of(k):
        both = rowbuf[pl.ds(pl.multiple_of(k * 2 * width, 2 * width), 2 * width), :]

        for p in range(npair):
            got = lax.dot_general(
                amp[p], both, (((1,), (1,)), ((), ())), preferred_element_type=F32
            ).astype(BF16)
            for c in range(2):
                half[k * 2 + c, 0:d, p * width : (p + 1) * width] = got[
                    :, c * width : (c + 1) * width
                ]

    amp_in.wait()
    row_mate(mate_i).wait_recv()
    half_of(chip)

    for o in range(1, ny):
        q = chip_at(-o) * 2 + core
        row_over(o, q).wait_recv()
        for s in range(1, nlo):
            row_beside(o, s, lo).start()
        row_fwd(o, 0, core).start()
    for o in range(1, ny):
        for s in range(1, nlo):
            row_beside(o, s, lo_at(-s)).wait_recv()
            row_fwd(o, s, core).start()

    def half_far(o, carry):
        for s in range(nlo):
            row_fwd(o, s, 1 - core).wait_recv()
        half_of(chip_at(-o))
        return carry

    lax.fori_loop(1, ny, half_far, 0)

    def x_send(t, s):
        return pltpu.make_async_remote_copy(
            src_ref=xs.at[t - 1, s - 1], dst_ref=xr.at[t - 1, s - 1],
            send_sem=xsem.at[0, t - 1, s - 1], recv_sem=xsem.at[1, t - 1, s - 1],
            device_id=beside(s), device_id_type=MESH,
        )

    def z_send(t):
        return pltpu.make_async_remote_copy(
            src_ref=zs.at[t - 1], dst_ref=zr.at[t - 1],
            send_sem=zsem.at[0, t - 1], recv_sem=zsem.at[1, t - 1],
            device_id=along(t), device_id_type=MESH,
        )

    def dot(q, b):
        return jnp.dot(pg[q, b], half[q], preferred_element_type=F32)

    def added(t):
        total = own[t - 1]
        for s in range(1, nlo):
            x_send(t, s).wait_recv()
            total = total + xr[t - 1, s - 1].astype(F32)
        return total

    def pass_on(t):
        zs[t - 1] = added(t).astype(BF16)
        z_send(t).start()

    def step(t, carry):
        for s in range(1, nlo + 1):
            b = block_of(t, s)
            for o in range(1, ny):
                q = chip_at(-o) * 2 + core
                pan_over(o, q, t, s).wait_recv()
                pan_fwd(o, core, t, s).start()
            pan_mate(mate_i, t, s).wait_recv()
            acc = dot(i, b) + dot(mate_i, b)
            for o in range(1, ny):
                acc = acc + dot(chip_at(-o) * 2 + core, b)
            for o in range(1, ny):
                pan_fwd(o, 1 - core, t, s).wait_recv()
                acc = acc + dot(chip_at(-o) * 2 + 1 - core, b)
            if s < nlo:
                xs[t - 1, s - 1] = acc.astype(BF16)
                x_send(t, s).start()
            else:
                own[t - 1] = acc

        @pl.when(t > 1)
        def _():
            pass_on(t - 1)

        return carry

    lax.fori_loop(1, nhi + 1, step, 0)

    total = added(nhi)
    for t in range(1, nhi):
        z_send(t).wait_recv()
        total = total + zr[t - 1].astype(F32)
    for p in range(npair):
        out[:, p, :] = total[:, p * width : (p + 1) * width]

    row_mate(i).wait_send()
    for o in range(1, ny):
        row_over(o, i).wait_send()
        row_fwd(o, 0, core).wait_send()
        for s in range(1, nlo):
            row_beside(o, s, lo).wait_send()
            row_fwd(o, s, core).wait_send()

    def drain(t, carry):
        for s in range(1, nlo + 1):
            pan_mate(i, t, s).wait_send()
            for o in range(1, ny):
                pan_over(o, i, t, s).wait_send()
                pan_fwd(o, core, t, s).wait_send()
            if s < nlo:
                x_send(t, s).wait_send()
        return carry

    lax.fori_loop(1, nhi + 1, drain, 0)
    for t in range(1, nhi):
        z_send(t).wait_send()


def on_device(na, nhi, nlo, row_codes, row_scales, panel_codes, panel_scales, amplitudes):
    npair, d, length = amplitudes.shape
    width = row_codes.shape[1]
    nw = nhi * nlo
    bw = length // nw
    dp = -(-d // 128) * 128
    ny = na // 2
    cols = npair * width
    dma = pltpu.SemaphoreType.DMA
    vmem = pl.BlockSpec(memory_space=pltpu.VMEM)
    return pl.pallas_call(
        functools.partial(kernel, na, nhi, nlo),
        out_shape=jax.ShapeDtypeStruct((bw, npair, width), F32),
        in_specs=[vmem, vmem, vmem, vmem, pl.BlockSpec(memory_space=pl.ANY)],
        out_specs=vmem,
        scratch_shapes=[
            pltpu.VMEM((na * width, length), BF16),
            pltpu.VMEM((na, nw, bw, dp), BF16),
            pltpu.VMEM((na, dp, cols), BF16),
            pltpu.VMEM((npair, d, length), BF16),
            pltpu.VMEM((nhi, bw, cols), F32),
            pltpu.VMEM((nhi, nlo - 1, bw, cols), BF16),
            pltpu.VMEM((nhi, nlo - 1, bw, cols), BF16),
            pltpu.VMEM((nhi - 1, bw, cols), BF16),
            pltpu.VMEM((nhi - 1, bw, cols), BF16),
            dma(()),
            dma((2,)),
            dma((2, ny)),
            dma((2, ny, nlo)),
            dma((2, ny, nlo)),
            dma((2, nw)),
            dma((2, ny, nw)),
            dma((2, ny, nw)),
            dma((2, nhi, nlo - 1)),
            dma((2, nhi - 1)),
        ],
        compiler_params=pltpu.CompilerParams(
            collective_id=0, has_side_effects=True, vmem_limit_bytes=56 * 1024 * 1024
        ),
        cost_estimate=pl.CostEstimate(
            flops=4 * npair * d * length * na * width,
            bytes_accessed=2 * npair * d * length,
            transcendentals=0,
        ),
    )(row_codes, row_scales, panel_codes, panel_scales, amplitudes)


def solution(mesh):
    na, nw = mesh.shape["aux"], mesh.shape["virt"]
    nlo = 4 if nw % 16 == 0 else 2
    placed = (
        P("aux", None, None),
        P("aux", None, None),
        P("aux", "virt", None),
        P("aux", "virt", None),
        P("aux", "virt", None),
    )
    return jax.shard_map(
        functools.partial(on_device, na, nw // nlo, nlo),
        mesh=mesh, in_specs=placed, out_specs=P("virt", "aux", None), check_vma=False,
    )
```

```python
import functools

import jax
import jax.numpy as jnp
from jax import lax
from jax.experimental import pallas as pl
from jax.experimental.pallas import tpu as pltpu
from jax.sharding import PartitionSpec as P

MESH = pl.DeviceIdType.MESH
BF16 = jnp.bfloat16
F32 = jnp.float32


def kernel(
    na, nhi, nlo,
    rowc, rows_, panc, pans, amp_hbm, out,
    rowbuf, pg, half, amp, own, xs, xr, zs, zr,
    amp_sem, row0, ry, rx, rm, pm, py, pf, xsem, zsem,
):
    npair, d, length = amp.shape
    width = rowc.shape[1]
    blocks = rows_.shape[0]
    blk = length // blocks
    dp = pg.shape[3]
    bw = pg.shape[2]
    ny = na // 2
    nw = nhi * nlo
    part = width // nlo
    subs = part // 16
    cuts = own.shape[1]
    cw = own.shape[3]

    i = lax.axis_index("aux")
    j = lax.axis_index("virt")
    chip, core = i // 2, i % 2
    hi, lo = j // nlo, j % nlo
    mate_i = chip * 2 + (1 - core)

    def chip_at(o):
        return lax.rem(chip + o + ny, ny)

    def lo_at(s):
        return lax.rem(lo + s + nlo, nlo)

    def hi_at(t):
        return lax.rem(hi + t + nhi, nhi)

    mate = (mate_i, j)

    def over(o):
        return (chip_at(o) * 2 + core, j)

    def beside(s):
        return (i, hi * nlo + lo_at(s))

    def along(t):
        return (i, hi_at(t) * nlo + lo)

    amp_in = pltpu.make_async_copy(amp_hbm, amp, amp_sem)
    amp_in.start()

    barrier = pltpu.get_barrier_semaphore()
    partners = [mate] + [over(o) for o in range(1, ny)]
    partners += [beside(s) for s in range(1, nlo)] + [along(t) for t in range(1, nhi)]
    for who in partners:
        pl.semaphore_signal(barrier, inc=1, device_id=who, device_id_type=MESH)

    by_row = rows_[:, 0, :].T
    my_row = pl.multiple_of(i * width, width)
    for k in range(blocks):
        at = slice(k * blk, (k + 1) * blk)
        rowbuf[pl.ds(my_row, width), at] = (
            rowc[0, :, at].astype(F32) * by_row[:, k : k + 1]
        ).astype(BF16)

    pl.semaphore_wait(barrier, len(partners))

    def send(ref, sems, who):
        return pltpu.make_async_remote_copy(
            src_ref=ref, dst_ref=ref, send_sem=sems[0], recv_sem=sems[1],
            device_id=who, device_id_type=MESH,
        )

    def piece(q, p, g):
        return rowbuf.at[pl.ds(pl.multiple_of(q * width + p * part + g * 16, 16), 16)]

    def row_mate(q):
        ref = rowbuf.at[pl.ds(pl.multiple_of(q * width, width), width)]
        return send(ref, (row0.at[0], row0.at[1]), mate)

    def row_over(o, q, g):
        return send(piece(q, lo, g), (ry.at[0, o, g], ry.at[1, o, g]), over(o))

    def row_beside(o, s, p, g):
        q = chip_at(-o) * 2 + core
        return send(piece(q, p, g), (rx.at[0, o, s, g], rx.at[1, o, s, g]), beside(s))

    def row_fwd(o, s, c, g):
        q = chip_at(-o) * 2 + c
        return send(piece(q, lo_at(-s), g), (rm.at[0, o, s, g], rm.at[1, o, s, g]), mate)

    for g in range(subs):
        for o in range(1, ny):
            row_over(o, i, g).start()
    row_mate(i).start()

    half[...] = jnp.zeros_like(half)
    for k in range(blocks):
        at = slice(k * blk, (k + 1) * blk)
        turned = panc[0, :, at].astype(F32).T * pans[k]
        if dp > d:
            turned = jnp.concatenate([turned, jnp.zeros((blk, dp - d), F32)], axis=1)
        first = k * blk
        while first < (k + 1) * blk:
            c = first // bw
            last = min((c + 1) * bw, (k + 1) * blk)
            pg[i, c, first - c * bw : last - c * bw, :] = turned[
                first - k * blk : last - k * blk
            ].astype(BF16)
            first = last

    def turn(n):
        if nhi < 3:
            return n
        if isinstance(n, int):
            return {1: 2, 2: 1}.get(n, n)
        return jnp.where(n == 1, 2, jnp.where(n == 2, 1, n))

    def block_of(n, s):
        return hi_at(turn(n)) * nlo + lo_at(s)

    def pan_mate(q, t, s):
        n = (t - 1) * nlo + (s - 1)
        return send(pg.at[q, block_of(t, s)], (pm.at[0, n], pm.at[1, n]), mate)

    def pan_over(o, q, t, s):
        n = (t - 1) * nlo + (s - 1)
        return send(pg.at[q, block_of(t, s)], (py.at[0, o, n], py.at[1, o, n]), over(o))

    def pan_fwd(o, c, t, s):
        n = (t - 1) * nlo + (s - 1)
        q = chip_at(-o) * 2 + c
        return send(pg.at[q, block_of(t, s)], (pf.at[0, o, n], pf.at[1, o, n]), mate)

    for t in range(1, nhi + 1):
        for s in range(1, nlo + 1):
            for o in range(1, ny):
                pan_over(o, i, t, s).start()
            pan_mate(i, t, s).start()

    def half_of(k):
        both = rowbuf[pl.ds(pl.multiple_of(k * 2 * width, 2 * width), 2 * width), :]

        for p in range(npair):
            got = lax.dot_general(
                amp[p], both, (((1,), (1,)), ((), ())), preferred_element_type=F32
            ).astype(BF16)
            for c in range(2):
                half[k * 2 + c, 0:d, p * width : (p + 1) * width] = got[
                    :, c * width : (c + 1) * width
                ]

    amp_in.wait()
    row_mate(mate_i).wait_recv()
    half_of(chip)

    for g in range(subs + 1):
        for o in range(1, ny):
            if g < subs:
                row_over(o, chip_at(-o) * 2 + core, g).wait_recv()
                for s in range(1, nlo):
                    row_beside(o, s, lo, g).start()
                row_fwd(o, 0, core, g).start()
            if g > 0:
                for s in range(1, nlo):
                    row_beside(o, s, lo_at(-s), g - 1).wait_recv()
                    row_fwd(o, s, core, g - 1).start()

    def half_far(o, carry):
        for s in range(nlo):
            for g in range(subs):
                row_fwd(o, s, 1 - core, g).wait_recv()
        half_of(chip_at(-o))
        return carry

    lax.fori_loop(1, ny, half_far, 0)

    def x_send(t, s, h):
        at = (t - 1, s - 1, h)
        return pltpu.make_async_remote_copy(
            src_ref=xs.at[at], dst_ref=xr.at[at],
            send_sem=xsem.at[(0,) + at], recv_sem=xsem.at[(1,) + at],
            device_id=beside(s), device_id_type=MESH,
        )

    def z_send(t, h):
        at = (t - 1, h)
        return pltpu.make_async_remote_copy(
            src_ref=zs.at[at], dst_ref=zr.at[at],
            send_sem=zsem.at[(0,) + at], recv_sem=zsem.at[(1,) + at],
            device_id=along(turn(t)), device_id_type=MESH,
        )

    def dot(q, b, h):
        return jnp.dot(
            pg[q, b], half[q, :, h * cw : (h + 1) * cw], preferred_element_type=F32
        )

    def partial(b, h):
        acc = dot(i, b, h) + dot(mate_i, b, h)
        for o in range(1, ny):
            for c in range(2):
                acc = acc + dot(chip_at(-o) * 2 + c, b, h)
        return acc

    def added(t, h):
        total = own[t - 1, h]
        for s in range(1, nlo):
            x_send(t, s, h).wait_recv()
            total = total + xr[t - 1, s - 1, h].astype(F32)
        return total

    def pass_on(t):
        for h in range(cuts):
            zs[t - 1, h] = added(t, h).astype(BF16)
            z_send(t, h).start()

    def step(t, carry):
        for s in range(1, nlo + 1):
            b = block_of(t, s)
            for o in range(1, ny):
                q = chip_at(-o) * 2 + core
                pan_over(o, q, t, s).wait_recv()
                pan_fwd(o, core, t, s).start()
            pan_mate(mate_i, t, s).wait_recv()
            for o in range(1, ny):
                pan_fwd(o, 1 - core, t, s).wait_recv()
            for h in range(cuts):
                if s < nlo:
                    xs[t - 1, s - 1, h] = partial(b, h).astype(BF16)
                    x_send(t, s, h).start()
                else:
                    own[t - 1, h] = partial(b, h)

        @pl.when(t > 1)
        def _():
            pass_on(t - 1)

        return carry

    lax.fori_loop(1, nhi + 1, step, 0)

    for h in range(cuts):
        total = added(nhi, h)
        for t in range(1, nhi):
            z_send(t, h).wait_recv()
            total = total + zr[t - 1, h].astype(F32)
        for p in range(cw // width):
            out[:, h * (cw // width) + p, :] = total[:, p * width : (p + 1) * width]

    row_mate(i).wait_send()
    for g in range(subs):
        for o in range(1, ny):
            row_over(o, i, g).wait_send()
            row_fwd(o, 0, core, g).wait_send()
            for s in range(1, nlo):
                row_beside(o, s, lo, g).wait_send()
                row_fwd(o, s, core, g).wait_send()

    def drain(t, carry):
        for s in range(1, nlo + 1):
            pan_mate(i, t, s).wait_send()
            for o in range(1, ny):
                pan_over(o, i, t, s).wait_send()
                pan_fwd(o, core, t, s).wait_send()
            if s < nlo:
                for h in range(cuts):
                    x_send(t, s, h).wait_send()
        return carry

    lax.fori_loop(1, nhi + 1, drain, 0)
    for t in range(1, nhi):
        for h in range(cuts):
            z_send(t, h).wait_send()


def on_device(na, nhi, nlo, row_codes, row_scales, panel_codes, panel_scales, amplitudes):
    npair, d, length = amplitudes.shape
    width = row_codes.shape[1]
    nw = nhi * nlo
    bw = length // nw
    dp = -(-d // 128) * 128
    ny = na // 2
    cols = npair * width
    subs = width // nlo // 16
    by_block = lambda scales: jnp.transpose(scales, (2, 0, 1))
    dma = pltpu.SemaphoreType.DMA
    vmem = pl.BlockSpec(memory_space=pltpu.VMEM)
    return pl.pallas_call(
        functools.partial(kernel, na, nhi, nlo),
        out_shape=jax.ShapeDtypeStruct((bw, npair, width), F32),
        in_specs=[vmem, vmem, vmem, vmem, pl.BlockSpec(memory_space=pl.ANY)],
        out_specs=vmem,
        scratch_shapes=[
            pltpu.VMEM((na * width, length), BF16),
            pltpu.VMEM((na, nw, bw, dp), BF16),
            pltpu.VMEM((na, dp, cols), BF16),
            pltpu.VMEM((npair, d, length), BF16),
            pltpu.VMEM((nhi, 2, bw, cols // 2), F32),
            pltpu.VMEM((nhi, nlo - 1, 2, bw, cols // 2), BF16),
            pltpu.VMEM((nhi, nlo - 1, 2, bw, cols // 2), BF16),
            pltpu.VMEM((nhi - 1, 2, bw, cols // 2), BF16),
            pltpu.VMEM((nhi - 1, 2, bw, cols // 2), BF16),
            dma(()),
            dma((2,)),
            dma((2, ny, subs)),
            dma((2, ny, nlo, subs)),
            dma((2, ny, nlo, subs)),
            dma((2, nw)),
            dma((2, ny, nw)),
            dma((2, ny, nw)),
            dma((2, nhi, nlo - 1, 2)),
            dma((2, nhi - 1, 2)),
        ],
        compiler_params=pltpu.CompilerParams(
            collective_id=0, has_side_effects=True, vmem_limit_bytes=56 * 1024 * 1024
        ),
        cost_estimate=pl.CostEstimate(
            flops=4 * npair * d * length * na * width,
            bytes_accessed=2 * npair * d * length,
            transcendentals=0,
        ),
    )(row_codes, by_block(row_scales), panel_codes, by_block(panel_scales), amplitudes)


def solution(mesh):
    na, nw = mesh.shape["aux"], mesh.shape["virt"]
    nlo = 4 if nw % 16 == 0 else 2
    placed = (
        P("aux", None, None),
        P("aux", None, None),
        P("aux", "virt", None),
        P("aux", "virt", None),
        P("aux", "virt", None),
    )
    return jax.shard_map(
        functools.partial(on_device, na, nw // nlo, nlo),
        mesh=mesh, in_specs=placed, out_specs=P("virt", "aux", None), check_vma=False,
    )
```

```python
import functools

import jax
import jax.numpy as jnp
from jax import lax
from jax.experimental import pallas as pl
from jax.experimental.pallas import tpu as pltpu
from jax.sharding import PartitionSpec as P

MESH = pl.DeviceIdType.MESH
BF16 = jnp.bfloat16
F32 = jnp.float32


def kernel(
    na, nhi, nlo,
    rowc, rows_, panc, pans, amp_hbm, out,
    rowbuf, pg, half, amp, own, xs, xr, zs, zr,
    amp_sem, row0, ry, rx, rm, pm, py, pf, xsem, zsem,
):
    npair, d, length = amp.shape
    width = rowc.shape[1]
    blocks = rows_.shape[0]
    blk = length // blocks
    dp = pg.shape[3]
    bw = pg.shape[2]
    ny = na // 2
    nw = nhi * nlo
    part = width // nlo
    subs = part // 16
    cuts = own.shape[1]
    cw = own.shape[3]

    i = lax.axis_index("aux")
    j = lax.axis_index("virt")
    chip, core = i // 2, i % 2
    hi, lo = j // nlo, j % nlo
    mate_i = chip * 2 + (1 - core)

    def chip_at(o):
        return lax.rem(chip + o + ny, ny)

    def lo_at(s):
        return lax.rem(lo + s + nlo, nlo)

    def hi_at(t):
        return lax.rem(hi + t + nhi, nhi)

    mate = (mate_i, j)

    def over(o):
        return (chip_at(o) * 2 + core, j)

    def beside(s):
        return (i, hi * nlo + lo_at(s))

    def along(t):
        return (i, hi_at(t) * nlo + lo)

    amp_in = pltpu.make_async_copy(amp_hbm, amp, amp_sem)
    amp_in.start()

    barrier = pltpu.get_barrier_semaphore()
    partners = [mate] + [over(o) for o in range(1, ny)]
    partners += [beside(s) for s in range(1, nlo)] + [along(t) for t in range(1, nhi)]
    for who in partners:
        pl.semaphore_signal(barrier, inc=1, device_id=who, device_id_type=MESH)

    by_row = rows_[:, 0, :].T
    my_row = pl.multiple_of(i * width, width)
    for k in range(blocks):
        at = slice(k * blk, (k + 1) * blk)
        rowbuf[pl.ds(my_row, width), at] = (
            rowc[0, :, at].astype(F32) * by_row[:, k : k + 1]
        ).astype(BF16)

    pl.semaphore_wait(barrier, len(partners))

    def send(ref, sems, who):
        return pltpu.make_async_remote_copy(
            src_ref=ref, dst_ref=ref, send_sem=sems[0], recv_sem=sems[1],
            device_id=who, device_id_type=MESH,
        )

    def piece(q, p, g):
        return rowbuf.at[pl.ds(pl.multiple_of(q * width + p * part + g * 16, 16), 16)]

    def row_mate(q):
        ref = rowbuf.at[pl.ds(pl.multiple_of(q * width, width), width)]
        return send(ref, (row0.at[0], row0.at[1]), mate)

    def row_over(o, q, g):
        return send(piece(q, lo, g), (ry.at[0, o, g], ry.at[1, o, g]), over(o))

    def row_beside(o, s, p, g):
        q = chip_at(-o) * 2 + core
        return send(piece(q, p, g), (rx.at[0, o, s, g], rx.at[1, o, s, g]), beside(s))

    def row_fwd(o, s, c, g):
        q = chip_at(-o) * 2 + c
        return send(piece(q, lo_at(-s), g), (rm.at[0, o, s, g], rm.at[1, o, s, g]), mate)

    for g in range(subs):
        for o in range(1, ny):
            row_over(o, i, g).start()
    row_mate(i).start()

    half[...] = jnp.zeros_like(half)
    for k in range(blocks):
        at = slice(k * blk, (k + 1) * blk)
        turned = panc[0, :, at].astype(F32).T * pans[k]
        if dp > d:
            turned = jnp.concatenate([turned, jnp.zeros((blk, dp - d), F32)], axis=1)
        first = k * blk
        while first < (k + 1) * blk:
            c = first // bw
            last = min((c + 1) * bw, (k + 1) * blk)
            pg[i, c, first - c * bw : last - c * bw, :] = turned[
                first - k * blk : last - k * blk
            ].astype(BF16)
            first = last

    def block_of(n, s):
        return hi_at(n) * nlo + lo_at(s)

    def pan_mate(q, t, s):
        n = (t - 1) * nlo + (s - 1)
        return send(pg.at[q, block_of(t, s)], (pm.at[0, n], pm.at[1, n]), mate)

    def pan_over(o, q, t, s):
        n = (t - 1) * nlo + (s - 1)
        return send(pg.at[q, block_of(t, s)], (py.at[0, o, n], py.at[1, o, n]), over(o))

    def pan_fwd(o, c, t, s):
        n = (t - 1) * nlo + (s - 1)
        q = chip_at(-o) * 2 + c
        return send(pg.at[q, block_of(t, s)], (pf.at[0, o, n], pf.at[1, o, n]), mate)

    for t in range(1, nhi + 1):
        for s in range(1, nlo + 1):
            for o in range(1, ny):
                pan_over(o, i, t, s).start()
            pan_mate(i, t, s).start()

    def half_of(k):
        both = rowbuf[pl.ds(pl.multiple_of(k * 2 * width, 2 * width), 2 * width), :]

        for p in range(npair):
            got = lax.dot_general(
                amp[p], both, (((1,), (1,)), ((), ())), preferred_element_type=F32
            ).astype(BF16)
            for c in range(2):
                half[k * 2 + c, 0:d, p * width : (p + 1) * width] = got[
                    :, c * width : (c + 1) * width
                ]

    amp_in.wait()
    row_mate(mate_i).wait_recv()
    half_of(chip)

    for g in range(subs + 1):
        for o in range(1, ny):
            if g < subs:
                row_over(o, chip_at(-o) * 2 + core, g).wait_recv()
                for s in range(1, nlo):
                    row_beside(o, s, lo, g).start()
                row_fwd(o, 0, core, g).start()
            if g > 0:
                for s in range(1, nlo):
                    row_beside(o, s, lo_at(-s), g - 1).wait_recv()
                    row_fwd(o, s, core, g - 1).start()

    def half_far(o, carry):
        for s in range(nlo):
            for g in range(subs):
                row_fwd(o, s, 1 - core, g).wait_recv()
        half_of(chip_at(-o))
        return carry

    lax.fori_loop(1, ny, half_far, 0)

    def x_send(t, s, h):
        at = (t - 1, s - 1, h)
        return pltpu.make_async_remote_copy(
            src_ref=xs.at[at], dst_ref=xr.at[at],
            send_sem=xsem.at[(0,) + at], recv_sem=xsem.at[(1,) + at],
            device_id=beside(s), device_id_type=MESH,
        )

    def z_send(t, h):
        at = (t - 1, h)
        return pltpu.make_async_remote_copy(
            src_ref=zs.at[at], dst_ref=zr.at[at],
            send_sem=zsem.at[(0,) + at], recv_sem=zsem.at[(1,) + at],
            device_id=along(t), device_id_type=MESH,
        )

    def dot(q, b, h):
        return jnp.dot(
            pg[q, b], half[q, :, h * cw : (h + 1) * cw], preferred_element_type=F32
        )

    def partial(b, h):
        acc = dot(i, b, h) + dot(mate_i, b, h)
        for o in range(1, ny):
            for c in range(2):
                acc = acc + dot(chip_at(-o) * 2 + c, b, h)
        return acc

    def added(t, h):
        total = own[t - 1, h]
        for s in range(1, nlo):
            x_send(t, s, h).wait_recv()
            total = total + xr[t - 1, s - 1, h].astype(F32)
        return total

    def pass_on(t):
        for h in range(cuts):
            zs[t - 1, h] = added(t, h).astype(BF16)
            z_send(t, h).start()

    def step(t, carry):
        for s in range(1, nlo + 1):
            b = block_of(t, s)
            for o in range(1, ny):
                q = chip_at(-o) * 2 + core
                pan_over(o, q, t, s).wait_recv()
                pan_fwd(o, core, t, s).start()
            pan_mate(mate_i, t, s).wait_recv()
            for o in range(1, ny):
                pan_fwd(o, 1 - core, t, s).wait_recv()
            for h in range(cuts):
                if s < nlo:
                    xs[t - 1, s - 1, h] = partial(b, h).astype(BF16)
                    x_send(t, s, h).start()
                else:
                    own[t - 1, h] = partial(b, h)

        @pl.when(t > 1)
        def _():
            pass_on(t - 1)

        return carry

    lax.fori_loop(1, nhi + 1, step, 0)

    for h in range(cuts):
        total = added(nhi, h)
        for t in range(1, nhi):
            z_send(t, h).wait_recv()
            total = total + zr[t - 1, h].astype(F32)
        for p in range(cw // width):
            out[:, h * (cw // width) + p, :] = total[:, p * width : (p + 1) * width]

    row_mate(i).wait_send()
    for g in range(subs):
        for o in range(1, ny):
            row_over(o, i, g).wait_send()
            row_fwd(o, 0, core, g).wait_send()
            for s in range(1, nlo):
                row_beside(o, s, lo, g).wait_send()
                row_fwd(o, s, core, g).wait_send()

    def drain(t, carry):
        for s in range(1, nlo + 1):
            pan_mate(i, t, s).wait_send()
            for o in range(1, ny):
                pan_over(o, i, t, s).wait_send()
                pan_fwd(o, core, t, s).wait_send()
            if s < nlo:
                for h in range(cuts):
                    x_send(t, s, h).wait_send()
        return carry

    lax.fori_loop(1, nhi + 1, drain, 0)
    for t in range(1, nhi):
        for h in range(cuts):
            z_send(t, h).wait_send()


def on_device(na, nhi, nlo, row_codes, row_scales, panel_codes, panel_scales, amplitudes):
    npair, d, length = amplitudes.shape
    width = row_codes.shape[1]
    nw = nhi * nlo
    bw = length // nw
    dp = -(-d // 128) * 128
    ny = na // 2
    cols = npair * width
    subs = width // nlo // 16
    by_block = lambda scales: jnp.transpose(scales, (2, 0, 1))
    dma = pltpu.SemaphoreType.DMA
    vmem = pl.BlockSpec(memory_space=pltpu.VMEM)
    return pl.pallas_call(
        functools.partial(kernel, na, nhi, nlo),
        out_shape=jax.ShapeDtypeStruct((bw, npair, width), F32),
        in_specs=[vmem, vmem, vmem, vmem, pl.BlockSpec(memory_space=pl.ANY)],
        out_specs=vmem,
        scratch_shapes=[
            pltpu.VMEM((na * width, length), BF16),
            pltpu.VMEM((na, nw, bw, dp), BF16),
            pltpu.VMEM((na, dp, cols), BF16),
            pltpu.VMEM((npair, d, length), BF16),
            pltpu.VMEM((nhi, 2, bw, cols // 2), F32),
            pltpu.VMEM((nhi, nlo - 1, 2, bw, cols // 2), BF16),
            pltpu.VMEM((nhi, nlo - 1, 2, bw, cols // 2), BF16),
            pltpu.VMEM((nhi - 1, 2, bw, cols // 2), BF16),
            pltpu.VMEM((nhi - 1, 2, bw, cols // 2), BF16),
            dma(()),
            dma((2,)),
            dma((2, ny, subs)),
            dma((2, ny, nlo, subs)),
            dma((2, ny, nlo, subs)),
            dma((2, nw)),
            dma((2, ny, nw)),
            dma((2, ny, nw)),
            dma((2, nhi, nlo - 1, 2)),
            dma((2, nhi - 1, 2)),
        ],
        compiler_params=pltpu.CompilerParams(
            collective_id=0, has_side_effects=True, vmem_limit_bytes=56 * 1024 * 1024
        ),
        cost_estimate=pl.CostEstimate(
            flops=4 * npair * d * length * na * width,
            bytes_accessed=2 * npair * d * length,
            transcendentals=0,
        ),
    )(row_codes, by_block(row_scales), panel_codes, by_block(panel_scales), amplitudes)


def solution(mesh):
    na, nw = mesh.shape["aux"], mesh.shape["virt"]
    nlo = 4 if nw % 16 == 0 else 2
    placed = (
        P("aux", None, None),
        P("aux", None, None),
        P("aux", "virt", None),
        P("aux", "virt", None),
        P("aux", "virt", None),
    )
    return jax.shard_map(
        functools.partial(on_device, na, nw // nlo, nlo),
        mesh=mesh, in_specs=placed, out_specs=P("virt", "aux", None), check_vma=False,
    )
```
